256 devices in a mesh: outer: 32 (over y_lo, z, core), inner: 8 (over y_hi, x).
Axes of the slice: x: 4, y: 4 (y_hi: 2, y_lo: 2; y = y_hi * 2 + y_lo), z: 8, core: 2. Of those that a mesh axis runs over, the one named last changes fastest.
Arguments:
- queries: bfloat16 [65536, 1024], P(('outer', 'inner')), may hold values from -1.6953125 to 1.6953125
- key_rows: bfloat16 [65536, 128], P(('outer', 'inner')), may hold values from -1.6953125 to 1.6953125
- value_rows: bfloat16 [65536, 128], P(('outer', 'inner')), may hold values from -6 to 6
- outputs: bfloat16 [65536, 1024], P(('outer', 'inner')), may hold values from -4 to 4
- out_grad: bfloat16 [65536, 1024], P(('outer', 'inner')), may hold values from -32 to 32
- log_norm: float32 [8, 65536], P(None, ('outer', 'inner')), may hold values from 6.5 to 8
- shard_pos: int32 [512], replicated, may hold values from 0 to 511, each once
Outputs:
- query_grad: bfloat16 [65536, 1024], P(('outer', 'inner'))
- key_grad: bfloat16 [65536, 128], P(('outer', 'inner'))
- value_grad: bfloat16 [65536, 128], P(('outer', 'inner'))
The draws below stay inside these ranges and needn't reach their ends.
Inputs may be any that keep to these rules, and one draw needn't show every extreme that they name: `shard_pos`: each of 0 to 511 appears once.
All inputs are finite; a program needn't handle non-finite values.
Results may differ from the reference program's by a relative error of at most 0.0049.
Values may be sent and summed in bfloat16 or wider, within the bound.
A program may use at most 128 MiB of HBM per device.

```python
from functools import partial
import jax
import jax.numpy as jnp
from jax import lax

HD = 128
HEADS = 8
SH = 128
OSTEPS = 6
ISTEPS = 2
SHARDS = 512
TOKENS = 65536
N_OUTER = 32
N_INNER = 8


def block_scale(rng, extent, cuts, low, high):
    factor_of = 1.0
    for position, blocks in cuts:
        steps = jax.random.uniform(jax.random.fold_in(jax.random.fold_in(rng, 6), position), (blocks,), jnp.float32, low / len(cuts), high / len(cuts))
        factor_of = factor_of * jnp.repeat(jnp.exp(steps), extent[position] // blocks).reshape((-1,) + (1,) * (len(extent) - 1 - position))
    return factor_of


def gaussian(key, extent, width, bound, shards=(), kind=jnp.bfloat16):
    values = jax.random.normal(key, extent, jnp.float32) * width
    if len(shards) > 0:
        values = block_scale(key, extent, shards, -0.22, 0.18) * values
    return jnp.clip(values, min=-bound, max=bound).astype(kind)


def setup_inputs(seed: int = 0) -> dict:
    arg_keys = jax.random.split(jax.random.key(seed), 8)
    queries = jnp.clip(jax.random.uniform(arg_keys[0], (TOKENS, HEADS * HD), jnp.float32, -1.6953125, 1.6953125) * block_scale(arg_keys[0], (TOKENS, HEADS * HD), ((0, 256),), -0.4, 0.0), -1.6953125, 1.6953125).astype(jnp.bfloat16)
    key_rows = jnp.clip(jax.random.uniform(arg_keys[1], (TOKENS, HD), jnp.float32, -1.6953125, 1.6953125) * block_scale(arg_keys[1], (TOKENS, HD), ((0, 256),), -0.4, 0.0), -1.6953125, 1.6953125).astype(jnp.bfloat16)
    value_rows = gaussian(arg_keys[2], (TOKENS, HD), 1.0, 6.0, ((0, 256),))
    outputs = gaussian(arg_keys[3], (TOKENS, HEADS * HD), 0.25, 4.0, ((0, 256),))
    out_grad = gaussian(arg_keys[4], (TOKENS, HEADS * HD), 6.0, 32.0, ((0, 256),))
    log_norm = jnp.clip(6.5 + 1.5 * jax.random.uniform(arg_keys[5], (HEADS, TOKENS), jnp.float32) ** block_scale(arg_keys[5], (HEADS, TOKENS), ((1, 256),), -0.2, 0.2), 6.5, 8.0)
    shard_pos = jax.random.permutation(arg_keys[6], SHARDS).astype(jnp.int32)
    return {"queries": queries, "key_rows": key_rows, "value_rows": value_rows, "outputs": outputs, "out_grad": out_grad, "log_norm": log_norm, "shard_pos": shard_pos}


def to_bfloat(source):
    return lax.optimization_barrier(source.astype(jnp.bfloat16)).astype(jnp.float32)


def block_grads(score_scale, members):
    query_heads, grad_heads, row_delta, norm_rows, query_pos, met_keys, met_values, met_pos = members
    scores = jnp.einsum("brhd,bcd->bhrc", query_heads, met_keys) * score_scale
    visible = met_pos[:, None, None, :] <= query_pos[:, None, :, None]
    weights = jnp.where(visible, jnp.exp(scores - norm_rows[:, :, :, None]), 0.0)
    weight_grad = jnp.einsum("brhd,bcd->bhrc", grad_heads, met_values)
    score_grad = to_bfloat(weights * (weight_grad - row_delta[:, :, :, None]) * score_scale)
    weights_low = to_bfloat(weights)
    query_part = jnp.einsum("bhrc,bcd->brhd", score_grad, met_keys)
    key_part = jnp.einsum("bhrc,brhd->bcd", score_grad, query_heads)
    value_part = jnp.einsum("bhrc,brhd->bcd", weights_low, grad_heads)
    return query_part, key_part, value_part


def reference(queries, key_rows, value_rows, outputs, out_grad, log_norm, shard_pos):
    row_count = 2 * SH
    score_scale = HD ** -0.5
    grid_shape = (N_OUTER, N_INNER, row_count)
    offsets = jnp.arange(SH, dtype=jnp.int32)
    positions = (shard_pos[:, None] * SH + offsets[None, :]).reshape(grid_shape)
    query_heads = queries.astype(jnp.float32).reshape(grid_shape + (HEADS, HD))
    grad_heads = out_grad.astype(jnp.float32).reshape(grid_shape + (HEADS, HD))
    output_heads = outputs.astype(jnp.float32).reshape(grid_shape + (HEADS, HD))
    key_grid = key_rows.astype(jnp.float32).reshape(grid_shape + (HD,))
    value_grid = value_rows.astype(jnp.float32).reshape(grid_shape + (HD,))
    row_delta = jnp.einsum("oirhd,oirhd->oihr", grad_heads, output_heads)
    norm_grid = jnp.transpose(log_norm.reshape(HEADS, N_OUTER, N_INNER, row_count), (1, 2, 0, 3))
    query_total = jnp.zeros(query_heads.shape, jnp.float32)
    key_total = jnp.zeros(key_grid.shape, jnp.float32)
    value_total = jnp.zeros(value_grid.shape, jnp.float32)
    for outer_step in range(OSTEPS):
        for inner_step in range(ISTEPS):
            shift_by = (outer_step, inner_step)
            met_keys = jnp.roll(key_grid, shift_by, axis=(0, 1))
            met_values = jnp.roll(value_grid, shift_by, axis=(0, 1))
            met_pos = jnp.roll(positions, shift_by, axis=(0, 1))
            members = tuple(jnp.moveaxis(member, 1, 0) for member in (query_heads, grad_heads, row_delta, norm_grid, positions, met_keys, met_values, met_pos))
            query_part, key_part, value_part = lax.map(partial(block_grads, score_scale), members)
            query_total = query_total + jnp.moveaxis(query_part, 0, 1)
            shift_back = (-outer_step, -inner_step)
            key_total = key_total + jnp.roll(jnp.moveaxis(key_part, 0, 1), shift_back, axis=(0, 1))
            value_total = value_total + jnp.roll(jnp.moveaxis(value_part, 0, 1), shift_back, axis=(0, 1))
    return (query_total.reshape(-1, HEADS * HD).astype(jnp.bfloat16), key_total.reshape(-1, HD).astype(jnp.bfloat16), value_total.reshape(-1, HD).astype(jnp.bfloat16))
```

```python
import functools

import jax
import jax.numpy as jnp
from jax import lax
from jax.experimental import pallas as pl
from jax.experimental.pallas import tpu as pltpu
from jax.sharding import PartitionSpec as P

F32 = jnp.float32
BF16 = jnp.bfloat16
MESH = pl.DeviceIdType.MESH
LOG2E = 1.4426950408889634
HIDDEN = 1e30

FAR = -1
STEPS = (
    (0, 0, 0),
    (1, 0, 0),
    (1, 0, 1),
    (0, 1, 0),
    (1, 1, 0),
    (1, 1, 1),
    (2, 0, 0),
    (2, 0, 1),
    (2, 1, 0),
    (2, 1, 1),
    (FAR, 1, 1),
    (FAR, 0, 1),
)


def dot(a, b):
    return jnp.dot(a, b, preferred_element_type=F32)


def dot_nt(a, b):
    return lax.dot_general(a, b, (((1,), (1,)), ((), ())), preferred_element_type=F32)


def at_step(t, values):
    return sum(jnp.where(t == n, value, 0) for n, value in enumerate(values))


def kernel(
    sizes,
    q_hbm, k_hbm, v_hbm, o_hbm, g_hbm, norm_hbm, pos_ref,
    dq_out, dk_out, dv_out,
    qs, gs, os, qt, gt, kv, norm, cols, cols_in, lse, delta, hidden,
    dq, dkv, staged, from_x, from_z, dq_send, dq_recv, dq_final, dkv_final,
    load_q, load_g, load_o, load_kv, load_norm, store_dq, store_dkv,
    swap_send, swap_recv, fwd_send, fwd_recv, ret_send, x_recv, z_recv,
):
    n_outer, n_inner, heads, rows, hd = sizes
    shard = rows // 2
    scale = hd**-0.5
    outer, inner = lax.axis_index("outer"), lax.axis_index("inner")
    core = lax.rem(outer, 2)

    def chip(dc, e=0):
        return (
            lax.rem(outer + 2 * dc + n_outer, n_outer),
            lax.rem(inner + e + n_inner, n_inner),
        )

    sibling = (outer + 1 - 2 * core, inner)

    def remote(src, dst, send, recv, to):
        return pltpu.make_async_remote_copy(
            src_ref=src, dst_ref=dst, send_sem=send, recv_sem=recv,
            device_id=to, device_id_type=MESH,
        )

    def loads(src, dst, sem):
        return [
            pltpu.make_async_copy(
                src.at[:, pl.ds(h * hd, hd)], dst.at[pl.ds(h * rows, rows)], sem.at[h]
            )
            for h in range(heads)
        ]

    kv_loads = [
        pltpu.make_async_copy(ref, kv.at[0, n], load_kv.at[n])
        for n, ref in enumerate((k_hbm, v_hbm))
    ]
    norm_load = pltpu.make_async_copy(norm_hbm, norm, load_norm)
    q_loads = loads(q_hbm, qs.at[0], load_q)
    g_loads = loads(g_hbm, gs.at[0], load_g)
    o_loads = loads(o_hbm, os, load_o)

    swap_q = remote(qs.at[0], qs.at[1], swap_send.at[0], swap_recv.at[0], sibling)
    swap_g = remote(gs.at[0], gs.at[1], swap_send.at[1], swap_recv.at[1], sibling)
    swap_cols = remote(cols, cols_in, swap_send.at[2], swap_recv.at[2], sibling)
    swap_dq = remote(dq_send, dq_recv, swap_send.at[3], swap_recv.at[3], sibling)

    def to_z(dc):
        return remote(
            kv.at[2 * dc], kv.at[2 * dc + 2], fwd_send.at[2 * dc], fwd_recv.at[2 * dc + 2], chip(1)
        )

    def to_x(dc):
        return remote(
            kv.at[2 * dc], kv.at[2 * dc + 1], fwd_send.at[2 * dc + 1], fwd_recv.at[2 * dc + 1],
            chip(0, 1),
        )

    def back_x(dc):
        slot = 2 * dc + 1
        return remote(
            staged.at[slot], from_x.at[dc], ret_send.at[slot], x_recv.at[dc], chip(0, -1)
        )

    def back_z(dc):
        slot = 2 * dc
        return remote(
            staged.at[slot], from_z.at[dc], ret_send.at[slot], z_recv.at[dc], chip(-dc)
        )

    for copy in (*kv_loads, *q_loads, *g_loads, norm_load, *o_loads):
        copy.start()
    partners = [sibling, chip(0, 1), chip(0, -1)]
    for dc in (1, 2, 3):
        partners += [chip(dc), chip(-dc)]
    barrier = pltpu.get_barrier_semaphore()
    for partner in partners:
        pl.semaphore_signal(barrier, inc=1, device_id=partner, device_id_type=MESH)

    dkv[...] = jnp.zeros_like(dkv)
    dq[...] = jnp.zeros_like(dq)
    for copy in kv_loads:
        copy.wait()
    pl.semaphore_wait(barrier, len(partners))
    to_z(0).start()
    to_x(0).start()
    for copy in q_loads:
        copy.wait()
    swap_q.start()
    for copy in g_loads:
        copy.wait()
    swap_g.start()

    norm_load.wait()
    lane = lax.broadcasted_iota(jnp.int32, (rows, hd), 1)
    padded = jnp.concatenate([norm[...] * LOG2E, jnp.zeros((hd - heads, rows), F32)], 0)
    cols[0] = padded.T
    for copy in o_loads:
        copy.wait()
    packed = jnp.zeros((rows, hd), F32)
    for h in range(heads):
        part = pl.ds(h * rows, rows)
        product = gs[0, part, :].astype(F32) * os[part, :].astype(F32)
        packed = jnp.where(lane == h, jnp.sum(product, axis=1, keepdims=True), packed)
    cols[1] = packed
    swap_cols.start()

    def prepare(side, source):
        for h in range(heads):
            part = pl.ds(h * rows, rows)
            lse[side, part, :] = jnp.broadcast_to(source[0, :, h : h + 1], (rows, hd))
            delta[side, part, :] = jnp.broadcast_to(source[1, :, h : h + 1], (rows, hd))
            qt[side, :, part] = qs[side, part, :].T
            gt[side, :, part] = gs[side, part, :].T

    prepare(0, cols)

    def positions(outer_index, inner_index, dim):
        first = 2 * (outer_index * n_inner + inner_index)
        at = lax.broadcasted_iota(jnp.int32, (rows, rows), dim)
        start = jnp.where(at < shard, pos_ref[first], pos_ref[first + 1] - 1)
        return start * shard + at

    chunk = heads * rows // 2

    def step(side, dc, e):
        slot = 2 * dc + e
        q_pos = positions(outer + side * (1 - 2 * core), inner, 0)
        kv_outer, kv_inner = chip(-dc, -e)
        k_pos = positions(kv_outer, kv_inner, 1)
        hidden[...] = jnp.where(k_pos <= q_pos, 0.0, HIDDEN)
        k, v = kv[slot, 0], kv[slot, 1]

        def front(j):
            part = pl.ds(j * chunk, chunk)
            return dot_nt(qs[side, part, :], k), dot_nt(gs[side, part, :], v)

        def middle(j, s, dp):
            part = pl.ds(j * chunk, chunk)
            row_lse = jnp.tile(lse[side, part, :], (1, rows // hd))
            row_delta = jnp.tile(delta[side, part, :], (1, rows // hd))
            exponent = s * (scale * LOG2E) - row_lse
            exponent = exponent.reshape(-1, rows, rows) - hidden[...][None]
            weights = jnp.exp2(exponent.reshape(chunk, rows))
            score_grad = weights * (dp - row_delta) * scale
            return weights.astype(BF16), score_grad.astype(BF16)

        def back(j, weights, score_grad):
            part = pl.ds(j * chunk, chunk)
            dq[side, part, :] += dot(score_grad, k)
            return dot(qt[side, :, part], score_grad), dot(gt[side, :, part], weights)

        ahead = front(0)
        dk = dv = None
        for j in range(2):
            now, ahead = ahead, front(1) if j == 0 else None
            dk_part, dv_part = back(j, *middle(j, *now))
            dk, dv = (dk_part, dv_part) if j == 0 else (dk + dk_part, dv + dv_part)
        dkv[slot, 0] += dk
        dkv[slot, 1] += dv

    far = 3 * core

    def on_far(body):
        pl.when(core == 1)(body)

    def send_x(dc):
        staged[2 * dc + 1] = dkv[2 * dc + 1].astype(BF16)
        back_x(dc).start()

    def send_z(dc):
        back_x(dc).wait_recv()
        staged[2 * dc] = (dkv[2 * dc] + from_x[dc].astype(F32)).astype(BF16)
        back_z(dc).start()

    def before(t):
        @pl.when(t == 1)
        def _():
            to_z(0).wait_recv()
            to_z(1).start()
            to_x(1).start()
            swap_q.wait_recv()
            swap_g.wait_recv()
            swap_cols.wait_recv()
            prepare(1, cols_in)

        @pl.when(t == 3)
        def _():
            to_x(0).wait_recv()

        @pl.when(t == 4)
        def _():
            to_z(1).wait_recv()
            on_far(lambda: to_z(2).start())
            to_x(2).start()
            to_x(1).wait_recv()

        @pl.when((t == 7) & (core == 1))
        def _():
            to_z(2).wait_recv()
            to_x(3).start()

        @pl.when(t == 8)
        def _():
            to_x(2).wait_recv()

        @pl.when((t == 10) & (core == 1))
        def _():
            to_x(3).wait_recv()

    def after(t):
        @pl.when(t == 5)
        def _():
            send_x(1)

        @pl.when(t == 7)
        def _():
            send_z(1)

        @pl.when(t == 9)
        def _():
            send_x(2)

        @pl.when(t == 10)
        def _():
            send_x(0)
            on_far(lambda: send_x(3))

    def body(t, carry):
        before(t)
        dc = at_step(t, [far if dc == FAR else dc for dc, _, _ in STEPS])
        e = at_step(t, [e for _, e, _ in STEPS])
        side = at_step(t, [side for _, _, side in STEPS])
        step(side, dc, e)
        after(t)
        return carry

    lax.fori_loop(0, len(STEPS), body, 0)

    dq_send[...] = dq[1].astype(BF16)
    swap_dq.start()
    send_z(2)
    on_far(lambda: send_z(3))

    swap_dq.wait_recv()
    stores = []
    for h in range(heads):
        part = pl.ds(h * rows, rows)
        dq_final[part, :] = (dq[0, part, :] + dq_recv[part, :].astype(F32)).astype(BF16)
        copy = pltpu.make_async_copy(
            dq_final.at[part], dq_out.at[:, pl.ds(h * hd, hd)], store_dq.at[h]
        )
        copy.start()
        stores.append(copy)

    back_x(0).wait_recv()
    back_z(1).wait_recv()
    dkv[0] += from_x[0].astype(F32) + from_z[1].astype(F32)
    back_z(2).wait_recv()
    dkv[0] += from_z[2].astype(F32)

    @pl.when(core == 1)
    def _():
        back_z(3).wait_recv()
        dkv[0] += from_z[3].astype(F32)

    dkv_final[0] = dkv[0, 0].T.astype(BF16)
    dkv_final[1] = dkv[0, 1].T.astype(BF16)
    for n, ref in enumerate((dk_out, dv_out)):
        copy = pltpu.make_async_copy(dkv_final.at[n], ref, store_dkv.at[n])
        copy.start()
        stores.append(copy)

    for copy in (swap_q, swap_g, swap_cols, swap_dq):
        copy.wait_send()
    for copy in (to_z(0), to_z(1), to_x(0), to_x(1), to_x(2)):
        copy.wait_send()
    for copy in (back_x(0), back_x(1), back_x(2), back_z(1), back_z(2)):
        copy.wait_send()

    @pl.when(core == 1)
    def _():
        for copy in (to_z(2), to_x(3), back_x(3), back_z(3)):
            copy.wait_send()

    for copy in stores:
        copy.wait()


def local(mesh, queries, key_rows, value_rows, outputs, out_grad, log_norm, shard_pos):
    rows, hd = key_rows.shape
    heads = queries.shape[1] // hd
    flat = heads * rows
    sizes = (mesh.shape["outer"], mesh.shape["inner"], heads, rows, hd)
    dma = pltpu.SemaphoreType.DMA
    scratch = [
        pltpu.VMEM((2, flat, hd), BF16),
        pltpu.VMEM((2, flat, hd), BF16),
        pltpu.VMEM((flat, hd), BF16),
        pltpu.VMEM((2, hd, flat), BF16),
        pltpu.VMEM((2, hd, flat), BF16),
        pltpu.VMEM((8, 2, rows, hd), BF16),
        pltpu.VMEM((heads, rows), F32),
        pltpu.VMEM((2, rows, hd), F32),
        pltpu.VMEM((2, rows, hd), F32),
        pltpu.VMEM((2, flat, hd), F32),
        pltpu.VMEM((2, flat, hd), F32),
        pltpu.VMEM((rows, rows), F32),
        pltpu.VMEM((2, flat, hd), F32),
        pltpu.VMEM((8, 2, hd, rows), F32),
        pltpu.VMEM((8, 2, hd, rows), BF16),
        pltpu.VMEM((4, 2, hd, rows), BF16),
        pltpu.VMEM((4, 2, hd, rows), BF16),
        pltpu.VMEM((flat, hd), BF16),
        pltpu.VMEM((flat, hd), BF16),
        pltpu.VMEM((flat, hd), BF16),
        pltpu.VMEM((2, rows, hd), BF16),
        dma((heads,)),
        dma((heads,)),
        dma((heads,)),
        dma((2,)),
        dma,
        dma((heads,)),
        dma((2,)),
        dma((4,)),
        dma((4,)),
        dma((8,)),
        dma((8,)),
        dma((8,)),
        dma((4,)),
        dma((4,)),
    ]
    hbm = pl.BlockSpec(memory_space=pl.ANY)
    return pl.pallas_call(
        functools.partial(kernel, sizes),
        out_shape=(
            jax.ShapeDtypeStruct(queries.shape, BF16),
            jax.ShapeDtypeStruct(key_rows.shape, BF16),
            jax.ShapeDtypeStruct(value_rows.shape, BF16),
        ),
        in_specs=[hbm] * 6 + [pl.BlockSpec(memory_space=pltpu.SMEM)],
        out_specs=(hbm,) * 3,
        scratch_shapes=scratch,
        compiler_params=pltpu.CompilerParams(
            collective_id=0, has_side_effects=True, vmem_limit_bytes=48 * 2**20
        ),
        name="window_grads",
    )(queries, key_rows, value_rows, outputs, out_grad, log_norm, shard_pos)


def solution(mesh):
    rows = P(("outer", "inner"), None)
    return jax.shard_map(
        functools.partial(local, mesh),
        mesh=mesh,
        in_specs=(rows, rows, rows, rows, rows, P(None, ("outer", "inner")), P()),
        out_specs=(rows, rows, rows),
        check_vma=False,
    )
```

```python
import functools

import jax
import jax.numpy as jnp
from jax import lax
from jax.experimental import pallas as pl
from jax.experimental.pallas import tpu as pltpu
from jax.sharding import PartitionSpec as P

F32 = jnp.float32
BF16 = jnp.bfloat16
MESH = pl.DeviceIdType.MESH
LOG2E = 1.4426950408889634
HIDDEN = 1e30

FAR = -1
STEPS = (
    (1, 0, 0),
    (1, 0, 1),
    (2, 0, 1),
    (1, 1, 1),
    (1, 1, 0),
    (FAR, 1, 1),
    (2, 1, 1),
    (2, 1, 0),
    (FAR, 0, 1),
    (0, 1, 0),
    (2, 0, 0),
    (0, 0, 0),
)
EVENTS = {
    0: (("in 10", "in 01"),),
    1: (("swap",),),
    2: (("in 20", "out 10"),),
    3: (("in 11",),),
    5: (("out 11",), ("in 31", "out 11")),
    6: (("in 21",), ("in 21", "out 31")),
    8: (("out 21",), ("in 30", "out 21")),
    9: ((), ("out 30",)),
    10: (("out 01",),),
    11: (("out 20",),),
}
FORWARD = {
    "11": ("10", 0, 1),
    "20": ("10", 1, 0),
    "21": ("20", 0, 1),
    "30": ("20", 1, 0),
    "31": ("01", 3, 0),
}
RETURN = {
    "01": "home",
    "10": "home",
    "11": "z",
    "20": "home",
    "21": "x",
    "30": "z",
    "31": "x",
}


def dot(a, b):
    return jnp.dot(a, b, preferred_element_type=F32)


def dot_nt(a, b):
    return lax.dot_general(a, b, (((1,), (1,)), ((), ())), preferred_element_type=F32)


def at_step(t, values):
    return sum(jnp.where(t == n, value, 0) for n, value in enumerate(values))


def kernel(
    sizes,
    q_hbm, k_hbm, v_hbm, o_hbm, g_hbm, norm_hbm, pos_hbm,
    dq_out, dk_out, dv_out,
    qs, gs, os, qt, gt, kv, norm, cols, cols_in, lse, delta, hidden,
    dq, dkv, staged, merged, home, dq_send, dq_recv, dq_final, dkv_final, pos_ref,
    load_q, load_g, load_o, load_kv, load_norm, load_pos, store_dq, store_dkv,
    swap_send, swap_recv, fwd_send, fwd_recv, ret_send, merge_recv, home_recv,
):
    n_outer, n_inner, heads, rows, hd = sizes
    shard = rows // 2
    scale = hd**-0.5
    outer, inner = lax.axis_index("outer"), lax.axis_index("inner")
    core = lax.rem(outer, 2)
    on_core0 = pl.when(core == 0)
    on_core1 = pl.when(core == 1)

    def chip(dc, e=0):
        return (
            lax.rem(outer + 2 * dc + n_outer, n_outer),
            lax.rem(inner + e + n_inner, n_inner),
        )

    sibling = (outer + 1 - 2 * core, inner)

    def remote(src, dst, send, recv, to):
        return pltpu.make_async_remote_copy(
            src_ref=src, dst_ref=dst, send_sem=send, recv_sem=recv,
            device_id=to, device_id_type=MESH,
        )

    def loads(src, dst, sem):
        return [
            pltpu.make_async_copy(
                src.at[:, pl.ds(h * hd, hd)], dst.at[pl.ds(h * rows, rows)], sem.at[h]
            )
            for h in range(heads)
        ]

    kv_loads = [
        pltpu.make_async_copy(ref, kv.at[0, n], load_kv.at[n])
        for n, ref in enumerate((k_hbm, v_hbm))
    ]
    pos_load = pltpu.make_async_copy(pos_hbm, pos_ref, load_pos)
    norm_load = pltpu.make_async_copy(norm_hbm, norm, load_norm)
    q_loads = loads(q_hbm, qs.at[0], load_q)
    g_loads = loads(g_hbm, gs.at[0], load_g)
    o_loads = loads(o_hbm, os, load_o)

    swap_q = remote(qs.at[0], qs.at[1], swap_send.at[0], swap_recv.at[0], sibling)
    swap_g = remote(gs.at[0], gs.at[1], swap_send.at[1], swap_recv.at[1], sibling)
    swap_cols = remote(cols, cols_in, swap_send.at[2], swap_recv.at[2], sibling)
    swap_dq = remote(dq_send, dq_recv, swap_send.at[3], swap_recv.at[3], sibling)

    def slot_of(name):
        return 2 * int(name[0]) + int(name[1])

    def on_core(name):
        return on_core1 if name[0] == "3" else lambda body: body()

    sources = {"10": ("own", 1, 0), "01": ("own", 0, 1), **FORWARD}

    def forward(name):
        source, dc, e = sources[name]
        src, dst = 0 if source == "own" else slot_of(source), slot_of(name)
        return remote(kv.at[src], kv.at[dst], fwd_send.at[dst], fwd_recv.at[dst], chip(dc, e))

    def send_on(source):
        for name, (before, _, _) in sources.items():
            if before == source:
                on_core(name)(lambda name=name: forward(name).start())

    def arrival(ref, sem, slot):
        return remote(ref.at[slot], ref.at[slot], fwd_send.at[slot], sem.at[slot], sibling)

    def onto(name):
        return {"home": "00", "x": name[0] + "0", "z": str(int(name[0]) - 1) + name[1]}[RETURN[name]]

    def back(name):
        slot = slot_of(name)
        if RETURN[name] == "home":
            ref, sem, to = home, home_recv, chip(-int(name[0]), -int(name[1]))
        else:
            ref, sem, to = merged, merge_recv, chip(-1) if RETURN[name] == "z" else chip(0, -1)
        return remote(staged.at[slot], ref.at[slot], ret_send.at[slot], sem.at[slot], to)

    for copy in (*kv_loads, *q_loads, *g_loads, norm_load, pos_load, *o_loads):
        copy.start()
    barrier = pltpu.get_barrier_semaphore()

    def greet(device):
        pl.semaphore_signal(barrier, inc=1, device_id=device, device_id_type=MESH)

    greet(sibling)
    reached = sorted({(dc, e) for _, dc, e in sources.values()})
    for dc, e in reached:
        greet(chip(-dc, -e))

    dkv[...] = jnp.zeros_like(dkv)
    dq[...] = jnp.zeros_like(dq)
    for copy in kv_loads:
        copy.wait()
    pl.semaphore_wait(barrier, 1 + len(reached))
    send_on("own")
    for copy in q_loads:
        copy.wait()
    swap_q.start()
    for copy in g_loads:
        copy.wait()
    swap_g.start()

    norm_load.wait()
    pos_load.wait()
    lane = lax.broadcasted_iota(jnp.int32, (rows, hd), 1)
    padded = jnp.concatenate([norm[...] * LOG2E, jnp.zeros((hd - heads, rows), F32)], 0)
    cols[0] = padded.T
    for copy in o_loads:
        copy.wait()
    packed = jnp.zeros((rows, hd), F32)
    for h in range(heads):
        part = pl.ds(h * rows, rows)
        product = gs[0, part, :].astype(F32) * os[part, :].astype(F32)
        packed = jnp.where(lane == h, jnp.sum(product, axis=1, keepdims=True), packed)
    cols[1] = packed
    swap_cols.start()

    def prepare(side, source):
        for h in range(heads):
            part = pl.ds(h * rows, rows)
            lse[side, part, :] = jnp.broadcast_to(source[0, :, h : h + 1], (rows, hd))
            delta[side, part, :] = jnp.broadcast_to(source[1, :, h : h + 1], (rows, hd))
            qt[side, :, part] = qs[side, part, :].T
            gt[side, :, part] = gs[side, part, :].T

    prepare(0, cols)

    def positions(outer_index, inner_index, dim):
        first = 2 * (outer_index * n_inner + inner_index)
        at = lax.broadcasted_iota(jnp.int32, (rows, rows), dim)
        start = jnp.where(at < shard, pos_ref[first], pos_ref[first + 1] - 1)
        return start * shard + at

    chunk = heads * rows // 2

    def step(side, dc, e):
        slot = 2 * dc + e
        q_pos = positions(outer + side * (1 - 2 * core), inner, 0)
        kv_outer, kv_inner = chip(-dc, -e)
        k_pos = positions(kv_outer, kv_inner, 1)
        hidden[...] = jnp.where(k_pos <= q_pos, 0.0, HIDDEN)
        k, v = kv[slot, 0], kv[slot, 1]

        def front(j):
            part = pl.ds(j * chunk, chunk)
            return dot_nt(qs[side, part, :], k), dot_nt(gs[side, part, :], v)

        def middle(j, s, dp):
            part = pl.ds(j * chunk, chunk)
            row_lse = jnp.tile(lse[side, part, :], (1, rows // hd))
            row_delta = jnp.tile(delta[side, part, :], (1, rows // hd))
            exponent = s * (scale * LOG2E) - row_lse
            exponent = exponent.reshape(-1, rows, rows) - hidden[...][None]
            weights = jnp.exp2(exponent.reshape(chunk, rows))
            score_grad = weights * (dp - row_delta) * scale
            return weights.astype(BF16), score_grad.astype(BF16)

        def back(j, weights, score_grad):
            part = pl.ds(j * chunk, chunk)
            dq[side, part, :] += dot(score_grad, k)
            return dot(qt[side, :, part], score_grad), dot(gt[side, :, part], weights)

        ahead = front(0)
        dk = dv = None
        for j in range(2):
            now, ahead = ahead, front(1) if j == 0 else None
            dk_part, dv_part = back(j, *middle(j, *now))
            dk, dv = (dk_part, dv_part) if j == 0 else (dk + dk_part, dv + dv_part)
        dkv[slot, 0] += dk
        dkv[slot, 1] += dv

    far = 3 * core

    def act(what):
        if what == "swap":
            swap_q.wait_recv()
            swap_g.wait_recv()
            swap_cols.wait_recv()
            prepare(1, cols_in)
            return
        kind, name = what.split()
        slot = slot_of(name)
        if kind == "in":
            arrival(kv, fwd_recv, slot).wait_recv()
            send_on(name)
            return
        for other in [other for other in RETURN if onto(other) == name]:

            @on_core(other)
            def _(other=slot_of(other)):
                arrival(merged, merge_recv, other).wait_recv()
                dkv[slot] += merged[other].astype(F32)

        staged[slot] = dkv[slot].astype(BF16)
        back(name).start()

    def events_at(n, here):
        if n not in EVENTS:
            return
        by_core = EVENTS[n]
        if len(by_core) == 1:
            pl.when(here)(lambda: [act(what) for what in by_core[0]] and None)
            return
        for index, events in enumerate(by_core):
            if events:
                pl.when(here & (core == index))(
                    lambda events=events: [act(what) for what in events] and None
                )

    def body(t, carry):
        for n in range(len(STEPS)):
            events_at(n, t == n)
        dc = at_step(t, [far if dc == FAR else dc for dc, _, _ in STEPS])
        e = at_step(t, [e for _, e, _ in STEPS])
        side = at_step(t, [side for _, _, side in STEPS])
        step(side, dc, e)
        return carry

    lax.fori_loop(0, len(STEPS), body, 0)

    dq_send[...] = dq[1].astype(BF16)
    swap_dq.start()
    events_at(len(STEPS), core >= 0)

    swap_dq.wait_recv()
    stores = []
    for h in range(heads):
        part = pl.ds(h * rows, rows)
        dq_final[part, :] = (dq[0, part, :] + dq_recv[part, :].astype(F32)).astype(BF16)
        copy = pltpu.make_async_copy(
            dq_final.at[part], dq_out.at[:, pl.ds(h * hd, hd)], store_dq.at[h]
        )
        copy.start()
        stores.append(copy)

    for name in RETURN:
        if RETURN[name] == "home":

            @on_core(name)
            def _(slot=slot_of(name)):
                arrival(home, home_recv, slot).wait_recv()
                dkv[0] += home[slot].astype(F32)

    dkv_final[0] = dkv[0, 0].T.astype(BF16)
    dkv_final[1] = dkv[0, 1].T.astype(BF16)
    for n, ref in enumerate((dk_out, dv_out)):
        copy = pltpu.make_async_copy(dkv_final.at[n], ref, store_dkv.at[n])
        copy.start()
        stores.append(copy)

    for copy in (swap_q, swap_g, swap_cols, swap_dq):
        copy.wait_send()
    for name in sources:

        @on_core(name)
        def _(name=name):
            forward(name).wait_send()
            back(name).wait_send()

    for copy in stores:
        copy.wait()


def store(*refs):
    bufs, sems = refs[6:9], refs[9]
    into = [pltpu.make_async_copy(refs[n], bufs[n], sems.at[n]) for n in range(3)]
    out = [pltpu.make_async_copy(bufs[n], refs[3 + n], sems.at[3 + n]) for n in range(3)]
    for copy in into:
        copy.start()
    for n in range(3):
        into[n].wait()
        out[n].start()
    for copy in out:
        copy.wait()


def local(mesh, queries, key_rows, value_rows, outputs, out_grad, log_norm, shard_pos):
    rows, hd = key_rows.shape
    heads = queries.shape[1] // hd
    flat = heads * rows
    sizes = (mesh.shape["outer"], mesh.shape["inner"], heads, rows, hd)
    dma = pltpu.SemaphoreType.DMA
    scratch = [
        pltpu.VMEM((2, flat, hd), BF16),
        pltpu.VMEM((2, flat, hd), BF16),
        pltpu.VMEM((flat, hd), BF16),
        pltpu.VMEM((2, hd, flat), BF16),
        pltpu.VMEM((2, hd, flat), BF16),
        pltpu.VMEM((8, 2, rows, hd), BF16),
        pltpu.VMEM((heads, rows), F32),
        pltpu.VMEM((2, rows, hd), F32),
        pltpu.VMEM((2, rows, hd), F32),
        pltpu.VMEM((2, flat, hd), F32),
        pltpu.VMEM((2, flat, hd), F32),
        pltpu.VMEM((rows, rows), F32),
        pltpu.VMEM((2, flat, hd), F32),
        pltpu.VMEM((8, 2, hd, rows), F32),
        pltpu.VMEM((8, 2, hd, rows), BF16),
        pltpu.VMEM((8, 2, hd, rows), BF16),
        pltpu.VMEM((8, 2, hd, rows), BF16),
        pltpu.VMEM((flat, hd), BF16),
        pltpu.VMEM((flat, hd), BF16),
        pltpu.VMEM((flat, hd), BF16),
        pltpu.VMEM((2, rows, hd), BF16),
        pltpu.SMEM(shard_pos.shape, jnp.int32),
        dma((heads,)),
        dma((heads,)),
        dma((heads,)),
        dma((2,)),
        dma,
        dma,
        dma((heads,)),
        dma((2,)),
        dma((4,)),
        dma((4,)),
        dma((8,)),
        dma((8,)),
        dma((8,)),
        dma((8,)),
        dma((8,)),
    ]
    hbm = pl.BlockSpec(memory_space=pltpu.HBM)
    grads = pl.pallas_call(
        functools.partial(kernel, sizes),
        out_shape=(
            jax.ShapeDtypeStruct(queries.shape, BF16),
            jax.ShapeDtypeStruct(key_rows.shape, BF16),
            jax.ShapeDtypeStruct(value_rows.shape, BF16),
        ),
        in_specs=[hbm] * 7,
        out_specs=(hbm,) * 3,
        scratch_shapes=scratch,
        compiler_params=pltpu.CompilerParams(
            collective_id=0, has_side_effects=True, vmem_limit_bytes=63 * 2**20
        ),
        name="window_grads",
    )(queries, key_rows, value_rows, outputs, out_grad, log_norm, shard_pos)
    return pl.pallas_call(
        store,
        out_shape=[jax.ShapeDtypeStruct(grad.shape, grad.dtype) for grad in grads],
        in_specs=[hbm] * 3,
        out_specs=[hbm] * 3,
        scratch_shapes=[pltpu.VMEM(grad.shape, grad.dtype) for grad in grads] + [dma((6,))],
        name="store",
    )(*grads)


def solution(mesh):
    rows = P(("outer", "inner"), None)
    return jax.shard_map(
        functools.partial(local, mesh),
        mesh=mesh,
        in_specs=(rows, rows, rows, rows, rows, P(None, ("outer", "inner")), P()),
        out_specs=(rows, rows, rows),
        check_vma=False,
    )
```

```python
import functools

import jax
import jax.numpy as jnp
from jax import lax
from jax.experimental import pallas as pl
from jax.experimental.pallas import tpu as pltpu
from jax.sharding import PartitionSpec as P

F32 = jnp.float32
BF16 = jnp.bfloat16
MESH = pl.DeviceIdType.MESH
LOG2E = 1.4426950408889634
HIDDEN = 1e30

FAR = -1
STEPS = (
    (1, 0, 1),
    (2, 0, 0),
    (2, 0, 1),
    (1, 1, 1),
    (1, 1, 0),
    (2, 1, 0),
    (2, 1, 1),
    (1, 0, 0),
    (0, 1, 0),
    (FAR, 1, 1),
    (0, 0, 0),
    (FAR, 0, 1),
)
EVENTS = {
    0: (("in 10", "swap"),),
    1: (("in 20",),),
    3: (("in 11", "out 20"),),
    5: (("in 21", "out 11"),),
    6: (("in 01",),),
    7: (("out 21",),),
    8: (("out 10",), ("out 10", "in 31")),
    9: ((), ("out 01",)),
    10: (("out 01",), ("out 31",)),
    11: ((), ("in 30",)),
    12: ((), ("out 30",)),
}
FORWARD = {
    "11": ("10", 0, 1),
    "20": ("10", 1, 0),
    "21": ("20", 0, 1),
    "30": ("20", 1, 0),
    "31": ("21", 1, 0),
}
RETURN = {
    "01": "home",
    "10": "home",
    "11": "x",
    "20": "z",
    "21": "home",
    "30": "home",
    "31": "x",
}


def dot(a, b):
    return jnp.dot(a, b, preferred_element_type=F32)


def dot_nt(a, b):
    return lax.dot_general(a, b, (((1,), (1,)), ((), ())), preferred_element_type=F32)


def at_step(t, values):
    return sum(jnp.where(t == n, value, 0) for n, value in enumerate(values))


def kernel(
    sizes,
    q_hbm, k_hbm, v_hbm, o_hbm, g_hbm, norm_hbm, pos_hbm,
    dq_out, dk_out, dv_out,
    qs, gs, os, qt, gt, kv, norm, cols, cols_in, lse, delta, hidden,
    dq, dkv, staged, merged, home, dq_send, dq_recv, pos_ref,
    load_q, load_g, load_o, load_kv, load_norm, load_pos,
    swap_send, swap_recv, fwd_send, fwd_recv, ret_send, merge_recv, home_recv,
):
    n_outer, n_inner, heads, rows, hd = sizes
    shard = rows // 2
    scale = hd**-0.5
    outer, inner = lax.axis_index("outer"), lax.axis_index("inner")
    core = lax.rem(outer, 2)
    on_core0 = pl.when(core == 0)
    on_core1 = pl.when(core == 1)

    def chip(dc, e=0):
        return (
            lax.rem(outer + 2 * dc + n_outer, n_outer),
            lax.rem(inner + e + n_inner, n_inner),
        )

    sibling = (outer + 1 - 2 * core, inner)

    def remote(src, dst, send, recv, to):
        return pltpu.make_async_remote_copy(
            src_ref=src, dst_ref=dst, send_sem=send, recv_sem=recv,
            device_id=to, device_id_type=MESH,
        )

    def loads(src, dst, sem):
        return [
            pltpu.make_async_copy(
                src.at[:, pl.ds(h * hd, hd)], dst.at[pl.ds(h * rows, rows)], sem.at[h]
            )
            for h in range(heads)
        ]

    kv_loads = [
        pltpu.make_async_copy(ref, kv.at[0, n], load_kv.at[n])
        for n, ref in enumerate((k_hbm, v_hbm))
    ]
    pos_load = pltpu.make_async_copy(pos_hbm, pos_ref, load_pos)
    norm_load = pltpu.make_async_copy(norm_hbm, norm, load_norm)
    q_loads = loads(q_hbm, qs.at[0], load_q)
    g_loads = loads(g_hbm, gs.at[0], load_g)
    o_loads = loads(o_hbm, os, load_o)

    swap_q = remote(qs.at[0], qs.at[1], swap_send.at[0], swap_recv.at[0], sibling)
    swap_g = remote(gs.at[0], gs.at[1], swap_send.at[1], swap_recv.at[1], sibling)
    swap_cols = remote(cols, cols_in, swap_send.at[2], swap_recv.at[2], sibling)
    swap_dq = remote(dq_send, dq_recv, swap_send.at[3], swap_recv.at[3], sibling)

    def slot_of(name):
        return 2 * int(name[0]) + int(name[1])

    def on_core(name):
        return on_core1 if name[0] == "3" else lambda body: body()

    sources = {"10": ("own", 1, 0), "01": ("own", 0, 1), **FORWARD}

    def forward(name):
        source, dc, e = sources[name]
        src, dst = 0 if source == "own" else slot_of(source), slot_of(name)
        return remote(kv.at[src], kv.at[dst], fwd_send.at[dst], fwd_recv.at[dst], chip(dc, e))

    def send_on(source):
        for name, (before, _, _) in sources.items():
            if before == source:
                on_core(name)(lambda name=name: forward(name).start())

    def arrival(ref, sem, slot):
        return remote(ref.at[slot], ref.at[slot], fwd_send.at[slot], sem.at[slot], sibling)

    def onto(name):
        return {"home": "00", "x": name[0] + "0", "z": str(int(name[0]) - 1) + name[1]}[RETURN[name]]

    def back(name):
        slot = slot_of(name)
        if RETURN[name] == "home":
            ref, sem, to = home, home_recv, chip(-int(name[0]), -int(name[1]))
        else:
            ref, sem, to = merged, merge_recv, chip(-1) if RETURN[name] == "z" else chip(0, -1)
        return remote(staged.at[slot], ref.at[slot], ret_send.at[slot], sem.at[slot], to)

    for copy in (*kv_loads, *q_loads, *g_loads, norm_load, pos_load, *o_loads):
        copy.start()
    barrier = pltpu.get_barrier_semaphore()

    def greet(device):
        pl.semaphore_signal(barrier, inc=1, device_id=device, device_id_type=MESH)

    greet(sibling)
    reached = sorted({(dc, e) for _, dc, e in sources.values()})
    for dc, e in reached:
        greet(chip(-dc, -e))

    dkv[...] = jnp.zeros_like(dkv)
    dq[...] = jnp.zeros_like(dq)
    for copy in kv_loads:
        copy.wait()
    pl.semaphore_wait(barrier, 1 + len(reached))
    send_on("own")
    for copy in q_loads:
        copy.wait()
    swap_q.start()
    for copy in g_loads:
        copy.wait()
    swap_g.start()

    norm_load.wait()
    pos_load.wait()
    lane = lax.broadcasted_iota(jnp.int32, (rows, hd), 1)
    padded = jnp.concatenate([norm[...] * LOG2E, jnp.zeros((hd - heads, rows), F32)], 0)
    cols[0] = padded.T
    for copy in o_loads:
        copy.wait()
    packed = jnp.zeros((rows, hd), F32)
    for h in range(heads):
        part = pl.ds(h * rows, rows)
        product = gs[0, part, :].astype(F32) * os[part, :].astype(F32)
        packed = jnp.where(lane == h, jnp.sum(product, axis=1, keepdims=True), packed)
    cols[1] = packed
    swap_cols.start()

    def prepare(side, source):
        for h in range(heads):
            part = pl.ds(h * rows, rows)
            lse[side, part, :] = jnp.broadcast_to(source[0, :, h : h + 1], (rows, hd))
            delta[side, part, :] = jnp.broadcast_to(source[1, :, h : h + 1], (rows, hd))
            qt[side, :, part] = qs[side, part, :].T
            gt[side, :, part] = gs[side, part, :].T

    prepare(0, cols)

    def positions(outer_index, inner_index, dim):
        first = 2 * (outer_index * n_inner + inner_index)
        at = lax.broadcasted_iota(jnp.int32, (rows, rows), dim)
        start = jnp.where(at < shard, pos_ref[first], pos_ref[first + 1] - 1)
        return start * shard + at

    chunk = heads * rows // 2

    def step(side, dc, e):
        slot = 2 * dc + e
        q_pos = positions(outer + side * (1 - 2 * core), inner, 0)
        kv_outer, kv_inner = chip(-dc, -e)
        k_pos = positions(kv_outer, kv_inner, 1)
        hidden[...] = jnp.where(k_pos <= q_pos, 0.0, HIDDEN)
        k, v = kv[slot, 0], kv[slot, 1]

        def front(j):
            part = pl.ds(j * chunk, chunk)
            return dot_nt(qs[side, part, :], k), dot_nt(gs[side, part, :], v)

        def middle(j, s, dp):
            part = pl.ds(j * chunk, chunk)
            row_lse = jnp.tile(lse[side, part, :], (1, rows // hd))
            row_delta = jnp.tile(delta[side, part, :], (1, rows // hd))
            exponent = s * (scale * LOG2E) - row_lse
            exponent = exponent.reshape(-1, rows, rows) - hidden[...][None]
            weights = jnp.exp2(exponent.reshape(chunk, rows))
            score_grad = weights * (dp - row_delta) * scale
            return weights.astype(BF16), score_grad.astype(BF16)

        def back(j, weights, score_grad):
            part = pl.ds(j * chunk, chunk)
            dq[side, part, :] += dot(score_grad, k)
            return dot(qt[side, :, part], score_grad), dot(gt[side, :, part], weights)

        ahead = front(0)
        dk = dv = None
        for j in range(2):
            now, ahead = ahead, front(1) if j == 0 else None
            dk_part, dv_part = back(j, *middle(j, *now))
            dk, dv = (dk_part, dv_part) if j == 0 else (dk + dk_part, dv + dv_part)
        dkv[slot, 0] += dk
        dkv[slot, 1] += dv

    far = 3 * core

    def act(what):
        if what == "swap":
            swap_q.wait_recv()
            swap_g.wait_recv()
            swap_cols.wait_recv()
            prepare(1, cols_in)
            return
        kind, name = what.split()
        slot = slot_of(name)
        if kind == "in":
            arrival(kv, fwd_recv, slot).wait_recv()
            send_on(name)
            return
        for other in [other for other in RETURN if onto(other) == name]:

            @on_core(other)
            def _(other=slot_of(other)):
                arrival(merged, merge_recv, other).wait_recv()
                dkv[slot] += merged[other].astype(F32)

        staged[slot] = dkv[slot].astype(BF16)
        back(name).start()

    def events_at(n, here):
        if n not in EVENTS:
            return
        by_core = EVENTS[n]
        if len(by_core) == 1:
            pl.when(here)(lambda: [act(what) for what in by_core[0]] and None)
            return
        for index, events in enumerate(by_core):
            if events:
                pl.when(here & (core == index))(
                    lambda events=events: [act(what) for what in events] and None
                )

    def body(t, carry):
        for n in range(len(STEPS)):
            events_at(n, t == n)
        dc = at_step(t, [far if dc == FAR else dc for dc, _, _ in STEPS])
        e = at_step(t, [e for _, e, _ in STEPS])
        side = at_step(t, [side for _, _, side in STEPS])
        step(side, dc, e)
        return carry

    lax.fori_loop(0, len(STEPS), body, 0)

    dq_send[...] = dq[1].astype(BF16)
    swap_dq.start()
    events_at(len(STEPS), core >= 0)

    swap_dq.wait_recv()
    for h in range(heads):
        part = pl.ds(h * rows, rows)
        total = dq[0, part, :] + dq_recv[part, :].astype(F32)
        dq_out[:, h * hd : (h + 1) * hd] = total.astype(BF16)

    for name in RETURN:
        if RETURN[name] == "home":

            @on_core(name)
            def _(slot=slot_of(name)):
                arrival(home, home_recv, slot).wait_recv()
                dkv[0] += home[slot].astype(F32)

    dk_out[...] = dkv[0, 0].T.astype(BF16)
    dv_out[...] = dkv[0, 1].T.astype(BF16)

    for copy in (swap_q, swap_g, swap_cols, swap_dq):
        copy.wait_send()
    for name in sources:

        @on_core(name)
        def _(name=name):
            forward(name).wait_send()
            back(name).wait_send()


def store(*refs):
    copies = [
        pltpu.make_async_copy(refs[n], refs[3 + n], refs[6].at[n]) for n in range(3)
    ]
    for copy in copies:
        copy.start()
    for copy in copies:
        copy.wait()


def local(mesh, queries, key_rows, value_rows, outputs, out_grad, log_norm, shard_pos):
    rows, hd = key_rows.shape
    heads = queries.shape[1] // hd
    flat = heads * rows
    sizes = (mesh.shape["outer"], mesh.shape["inner"], heads, rows, hd)
    dma = pltpu.SemaphoreType.DMA
    scratch = [
        pltpu.VMEM((2, flat, hd), BF16),
        pltpu.VMEM((2, flat, hd), BF16),
        pltpu.VMEM((flat, hd), BF16),
        pltpu.VMEM((2, hd, flat), BF16),
        pltpu.VMEM((2, hd, flat), BF16),
        pltpu.VMEM((8, 2, rows, hd), BF16),
        pltpu.VMEM((heads, rows), F32),
        pltpu.VMEM((2, rows, hd), F32),
        pltpu.VMEM((2, rows, hd), F32),
        pltpu.VMEM((2, flat, hd), F32),
        pltpu.VMEM((2, flat, hd), F32),
        pltpu.VMEM((rows, rows), F32),
        pltpu.VMEM((2, flat, hd), F32),
        pltpu.VMEM((8, 2, hd, rows), F32),
        pltpu.VMEM((8, 2, hd, rows), BF16),
        pltpu.VMEM((8, 2, hd, rows), BF16),
        pltpu.VMEM((8, 2, hd, rows), BF16),
        pltpu.VMEM((flat, hd), BF16),
        pltpu.VMEM((flat, hd), BF16),
        pltpu.SMEM(shard_pos.shape, jnp.int32),
        dma((heads,)),
        dma((heads,)),
        dma((heads,)),
        dma((2,)),
        dma,
        dma,
        dma((4,)),
        dma((4,)),
        dma((8,)),
        dma((8,)),
        dma((8,)),
        dma((8,)),
        dma((8,)),
    ]
    hbm = pl.BlockSpec(memory_space=pltpu.HBM)
    vmem = pl.BlockSpec(memory_space=pltpu.VMEM)
    grads = pl.pallas_call(
        functools.partial(kernel, sizes),
        out_shape=(
            pltpu.VMEM(queries.shape, BF16),
            pltpu.VMEM(key_rows.shape, BF16),
            pltpu.VMEM(value_rows.shape, BF16),
        ),
        in_specs=[hbm] * 7,
        out_specs=(vmem,) * 3,
        scratch_shapes=scratch,
        compiler_params=pltpu.CompilerParams(
            collective_id=0, has_side_effects=True, vmem_limit_bytes=56 * 2**20
        ),
        name="window_grads",
    )(queries, key_rows, value_rows, outputs, out_grad, log_norm, shard_pos)
    return pl.pallas_call(
        store,
        out_shape=[jax.ShapeDtypeStruct(grad.shape, grad.dtype) for grad in grads],
        in_specs=[vmem] * 3,
        out_specs=[hbm] * 3,
        scratch_shapes=[dma((3,))],
        name="store",
    )(*(pltpu.with_memory_space_constraint(grad, pltpu.VMEM) for grad in grads))


def solution(mesh):
    rows = P(("outer", "inner"), None)
    return jax.shard_map(
        functools.partial(local, mesh),
        mesh=mesh,
        in_specs=(rows, rows, rows, rows, rows, P(None, ("outer", "inner")), P()),
        out_specs=(rows, rows, rows),
        check_vma=False,
    )
```

```python
import functools

import jax
import jax.numpy as jnp
from jax import lax
from jax.experimental import pallas as pl
from jax.experimental.pallas import tpu as pltpu
from jax.sharding import PartitionSpec as P

F32 = jnp.float32
BF16 = jnp.bfloat16
MESH = pl.DeviceIdType.MESH
LOG2E = 1.4426950408889634
HIDDEN = 1e30

FAR = -1
STEPS = (
    (0, 0, 0),
    (1, 0, 1),
    (2, 0, 0),
    (2, 0, 1),
    (1, 1, 0),
    (1, 1, 1),
    (2, 1, 0),
    (2, 1, 1),
    (0, 1, 0),
    (1, 0, 0),
    (FAR, 1, 1),
    (FAR, 0, 1),
)
EVENTS = {
    1: (("in 10", "swap"),),
    2: (("in 20",),),
    4: (("in 11", "out 20"),),
    6: (("in 21", "out 11"),),
    8: (("in 01", "out 21"),),
    10: (("out 10",), ("in 31", "out 10", "out 01")),
    11: (("out 01",), ("in 30", "out 31")),
    12: ((), ("out 30",)),
}
FORWARD = {
    "11": ("10", 0, 1),
    "20": ("10", 1, 0),
    "21": ("20", 0, 1),
    "30": ("20", 1, 0),
    "31": ("21", 1, 0),
}
RETURN = {
    "01": "home",
    "10": "home",
    "11": "x",
    "20": "z",
    "21": "home",
    "30": "home",
    "31": "x",
}


def dot(a, b):
    return jnp.dot(a, b, preferred_element_type=F32)


def dot_nt(a, b):
    return lax.dot_general(a, b, (((1,), (1,)), ((), ())), preferred_element_type=F32)


def at_step(t, values):
    return sum(jnp.where(t == n, value, 0) for n, value in enumerate(values))


def kernel(
    sizes,
    q_hbm, k_hbm, v_hbm, o_hbm, g_hbm, norm_hbm, pos_hbm,
    dq_out, dk_out, dv_out,
    qs, gs, os, qt, gt, kv, norm, cols, cols_in, lse, delta, hidden,
    dq, dkv, staged, merged, home, dq_send, dq_recv, pos_ref,
    load_q, load_g, load_o, load_kv, load_norm, load_pos,
    swap_send, swap_recv, fwd_send, fwd_recv, ret_send, merge_recv, home_recv,
):
    n_outer, n_inner, heads, rows, hd = sizes
    shard = rows // 2
    scale = hd**-0.5
    outer, inner = lax.axis_index("outer"), lax.axis_index("inner")
    core = lax.rem(outer, 2)
    on_core0 = pl.when(core == 0)
    on_core1 = pl.when(core == 1)

    def chip(dc, e=0):
        return (
            lax.rem(outer + 2 * dc + n_outer, n_outer),
            lax.rem(inner + e + n_inner, n_inner),
        )

    sibling = (outer + 1 - 2 * core, inner)

    def remote(src, dst, send, recv, to):
        return pltpu.make_async_remote_copy(
            src_ref=src, dst_ref=dst, send_sem=send, recv_sem=recv,
            device_id=to, device_id_type=MESH,
        )

    def loads(src, dst, sem):
        return [
            pltpu.make_async_copy(
                src.at[:, pl.ds(h * hd, hd)], dst.at[pl.ds(h * rows, rows)], sem.at[h]
            )
            for h in range(heads)
        ]

    kv_loads = [
        pltpu.make_async_copy(ref, kv.at[0, n], load_kv.at[n])
        for n, ref in enumerate((k_hbm, v_hbm))
    ]
    pos_load = pltpu.make_async_copy(pos_hbm, pos_ref, load_pos)
    norm_load = pltpu.make_async_copy(norm_hbm, norm, load_norm)
    q_loads = loads(q_hbm, qs.at[0], load_q)
    g_loads = loads(g_hbm, gs.at[0], load_g)
    o_loads = loads(o_hbm, os, load_o)

    swap_q = remote(qs.at[0], qs.at[1], swap_send.at[0], swap_recv.at[0], sibling)
    swap_g = remote(gs.at[0], gs.at[1], swap_send.at[1], swap_recv.at[1], sibling)
    swap_cols = remote(cols, cols_in, swap_send.at[2], swap_recv.at[2], sibling)
    swap_dq = remote(dq_send, dq_recv, swap_send.at[3], swap_recv.at[3], sibling)

    def slot_of(name):
        return 2 * int(name[0]) + int(name[1])

    def on_core(name):
        return on_core1 if name[0] == "3" else lambda body: body()

    sources = {"10": ("own", 1, 0), "01": ("own", 0, 1), **FORWARD}

    def forward(name):
        source, dc, e = sources[name]
        src, dst = 0 if source == "own" else slot_of(source), slot_of(name)
        return remote(kv.at[src], kv.at[dst], fwd_send.at[dst], fwd_recv.at[dst], chip(dc, e))

    def send_on(source):
        for name, (before, _, _) in sources.items():
            if before == source:
                on_core(name)(lambda name=name: forward(name).start())

    def send_own():
        for name, (before, dc, e) in sources.items():
            if before == "own":
                dst = slot_of(name)
                for n, ref in enumerate((k_hbm, v_hbm)):
                    remote(
                        ref, kv.at[dst, n], fwd_send.at[dst], fwd_recv.at[dst], chip(dc, e)
                    ).start()

    def arrival(ref, sem, slot):
        return remote(ref.at[slot], ref.at[slot], fwd_send.at[slot], sem.at[slot], sibling)

    def onto(name):
        return {"home": "00", "x": name[0] + "0", "z": str(int(name[0]) - 1) + name[1]}[RETURN[name]]

    def back(name):
        slot = slot_of(name)
        if RETURN[name] == "home":
            ref, sem, to = home, home_recv, chip(-int(name[0]), -int(name[1]))
        else:
            ref, sem, to = merged, merge_recv, chip(-1) if RETURN[name] == "z" else chip(0, -1)
        return remote(staged.at[slot], ref.at[slot], ret_send.at[slot], sem.at[slot], to)

    barrier = pltpu.get_barrier_semaphore()

    def greet(device):
        pl.semaphore_signal(barrier, inc=1, device_id=device, device_id_type=MESH)

    reached = sorted({(dc, e) for _, dc, e in sources.values()})
    for dc, e in reached:
        greet(chip(-dc, -e))
    greet(sibling)
    for copy in (*kv_loads, *q_loads, *g_loads):
        copy.start()
    pl.semaphore_wait(barrier, 1 + len(reached))
    send_own()
    for copy in kv_loads:
        copy.wait()
    for copy in (*o_loads, norm_load, pos_load):
        copy.start()
    for copy in q_loads:
        copy.wait()
    swap_q.start()
    for copy in g_loads:
        copy.wait()
    swap_g.start()
    dkv[...] = jnp.zeros_like(dkv)
    dq[...] = jnp.zeros_like(dq)

    norm_load.wait()
    pos_load.wait()
    lane = lax.broadcasted_iota(jnp.int32, (rows, hd), 1)
    padded = jnp.concatenate([norm[...] * LOG2E, jnp.zeros((hd - heads, rows), F32)], 0)
    cols[0] = padded.T
    for copy in o_loads:
        copy.wait()
    packed = jnp.zeros((rows, hd), F32)
    for h in range(heads):
        part = pl.ds(h * rows, rows)
        product = gs[0, part, :].astype(F32) * os[part, :].astype(F32)
        packed = jnp.where(lane == h, jnp.sum(product, axis=1, keepdims=True), packed)
    cols[1] = packed
    swap_cols.start()

    def prepare(side, source):
        for h in range(heads):
            part = pl.ds(h * rows, rows)
            lse[side, part, :] = jnp.broadcast_to(source[0, :, h : h + 1], (rows, hd))
            delta[side, part, :] = jnp.broadcast_to(source[1, :, h : h + 1], (rows, hd))
            qt[side, :, part] = qs[side, part, :].T
            gt[side, :, part] = gs[side, part, :].T

    prepare(0, cols)

    def positions(outer_index, inner_index, dim):
        first = 2 * (outer_index * n_inner + inner_index)
        at = lax.broadcasted_iota(jnp.int32, (rows, rows), dim)
        start = jnp.where(at < shard, pos_ref[first], pos_ref[first + 1] - 1)
        return start * shard + at

    chunk = heads * rows // 2

    def step(side, dc, e):
        slot = 2 * dc + e
        q_pos = positions(outer + side * (1 - 2 * core), inner, 0)
        kv_outer, kv_inner = chip(-dc, -e)
        k_pos = positions(kv_outer, kv_inner, 1)
        hidden[...] = jnp.where(k_pos <= q_pos, 0.0, HIDDEN)
        k, v = kv[slot, 0], kv[slot, 1]

        def front(j):
            part = pl.ds(j * chunk, chunk)
            return dot_nt(qs[side, part, :], k), dot_nt(gs[side, part, :], v)

        def middle(j, s, dp):
            part = pl.ds(j * chunk, chunk)
            row_lse = jnp.tile(lse[side, part, :], (1, rows // hd))
            row_delta = jnp.tile(delta[side, part, :], (1, rows // hd))
            exponent = s * (scale * LOG2E) - row_lse
            exponent = exponent.reshape(-1, rows, rows) - hidden[...][None]
            weights = jnp.exp2(exponent.reshape(chunk, rows))
            score_grad = weights * (dp - row_delta) * scale
            return weights.astype(BF16), score_grad.astype(BF16)

        def back(j, weights, score_grad):
            part = pl.ds(j * chunk, chunk)
            dq[side, part, :] += dot(score_grad, k)
            return dot(qt[side, :, part], score_grad), dot(gt[side, :, part], weights)

        ahead = front(0)
        dk = dv = None
        for j in range(2):
            now, ahead = ahead, front(1) if j == 0 else None
            dk_part, dv_part = back(j, *middle(j, *now))
            dk, dv = (dk_part, dv_part) if j == 0 else (dk + dk_part, dv + dv_part)
        dkv[slot, 0] += dk
        dkv[slot, 1] += dv

    far = 3 * core

    def act(what):
        if what == "swap":
            swap_q.wait_recv()
            swap_g.wait_recv()
            swap_cols.wait_recv()
            prepare(1, cols_in)
            return
        kind, name = what.split()
        slot = slot_of(name)
        if kind == "in":
            arrival(kv, fwd_recv, slot).wait_recv()
            send_on(name)
            return
        for other in [other for other in RETURN if onto(other) == name]:

            @on_core(other)
            def _(other=slot_of(other)):
                arrival(merged, merge_recv, other).wait_recv()
                dkv[slot] += merged[other].astype(F32)

        staged[slot] = dkv[slot].astype(BF16)
        back(name).start()

    def events_at(n, here):
        if n not in EVENTS:
            return
        by_core = EVENTS[n]
        if len(by_core) == 1:
            pl.when(here)(lambda: [act(what) for what in by_core[0]] and None)
            return
        for index, events in enumerate(by_core):
            if events:
                pl.when(here & (core == index))(
                    lambda events=events: [act(what) for what in events] and None
                )

    def body(t, carry):
        for n in range(len(STEPS)):
            events_at(n, t == n)
        dc = at_step(t, [far if dc == FAR else dc for dc, _, _ in STEPS])
        e = at_step(t, [e for _, e, _ in STEPS])
        side = at_step(t, [side for _, _, side in STEPS])
        step(side, dc, e)
        return carry

    lax.fori_loop(0, len(STEPS), body, 0)

    dq_send[...] = dq[1].astype(BF16)
    swap_dq.start()
    events_at(len(STEPS), core >= 0)

    swap_dq.wait_recv()
    for h in range(heads):
        part = pl.ds(h * rows, rows)
        total = dq[0, part, :] + dq_recv[part, :].astype(F32)
        dq_out[:, h * hd : (h + 1) * hd] = total.astype(BF16)

    for name in RETURN:
        if RETURN[name] == "home":

            @on_core(name)
            def _(slot=slot_of(name)):
                arrival(home, home_recv, slot).wait_recv()
                dkv[0] += home[slot].astype(F32)

    dk_out[...] = dkv[0, 0].T.astype(BF16)
    dv_out[...] = dkv[0, 1].T.astype(BF16)

    for copy in (swap_q, swap_g, swap_cols, swap_dq):
        copy.wait_send()
    for name in sources:

        @on_core(name)
        def _(name=name):
            forward(name).wait_send()
            back(name).wait_send()


def store(*refs):
    copies = [
        pltpu.make_async_copy(refs[n], refs[3 + n], refs[6].at[n]) for n in range(3)
    ]
    for copy in copies:
        copy.start()
    for copy in copies:
        copy.wait()


def local(mesh, queries, key_rows, value_rows, outputs, out_grad, log_norm, shard_pos):
    rows, hd = key_rows.shape
    heads = queries.shape[1] // hd
    flat = heads * rows
    sizes = (mesh.shape["outer"], mesh.shape["inner"], heads, rows, hd)
    dma = pltpu.SemaphoreType.DMA
    scratch = [
        pltpu.VMEM((2, flat, hd), BF16),
        pltpu.VMEM((2, flat, hd), BF16),
        pltpu.VMEM((flat, hd), BF16),
        pltpu.VMEM((2, hd, flat), BF16),
        pltpu.VMEM((2, hd, flat), BF16),
        pltpu.VMEM((8, 2, rows, hd), BF16),
        pltpu.VMEM((heads, rows), F32),
        pltpu.VMEM((2, rows, hd), F32),
        pltpu.VMEM((2, rows, hd), F32),
        pltpu.VMEM((2, flat, hd), F32),
        pltpu.VMEM((2, flat, hd), F32),
        pltpu.VMEM((rows, rows), F32),
        pltpu.VMEM((2, flat, hd), F32),
        pltpu.VMEM((8, 2, hd, rows), F32),
        pltpu.VMEM((8, 2, hd, rows), BF16),
        pltpu.VMEM((8, 2, hd, rows), BF16),
        pltpu.VMEM((8, 2, hd, rows), BF16),
        pltpu.VMEM((flat, hd), BF16),
        pltpu.VMEM((flat, hd), BF16),
        pltpu.SMEM(shard_pos.shape, jnp.int32),
        dma((heads,)),
        dma((heads,)),
        dma((heads,)),
        dma((2,)),
        dma,
        dma,
        dma((4,)),
        dma((4,)),
        dma((8,)),
        dma((8,)),
        dma((8,)),
        dma((8,)),
        dma((8,)),
    ]
    hbm = pl.BlockSpec(memory_space=pltpu.HBM)
    vmem = pl.BlockSpec(memory_space=pltpu.VMEM)
    grads = pl.pallas_call(
        functools.partial(kernel, sizes),
        out_shape=(
            pltpu.VMEM(queries.shape, BF16),
            pltpu.VMEM(key_rows.shape, BF16),
            pltpu.VMEM(value_rows.shape, BF16),
        ),
        in_specs=[hbm] * 7,
        out_specs=(vmem,) * 3,
        scratch_shapes=scratch,
        compiler_params=pltpu.CompilerParams(
            collective_id=0, has_side_effects=True, vmem_limit_bytes=56 * 2**20
        ),
        name="window_grads",
    )(queries, key_rows, value_rows, outputs, out_grad, log_norm, shard_pos)
    return pl.pallas_call(
        store,
        out_shape=[jax.ShapeDtypeStruct(grad.shape, grad.dtype) for grad in grads],
        in_specs=[vmem] * 3,
        out_specs=[hbm] * 3,
        scratch_shapes=[dma((3,))],
        name="store",
    )(*(pltpu.with_memory_space_constraint(grad, pltpu.VMEM) for grad in grads))


def solution(mesh):
    rows = P(("outer", "inner"), None)
    return jax.shard_map(
        functools.partial(local, mesh),
        mesh=mesh,
        in_specs=(rows, rows, rows, rows, rows, P(None, ("outer", "inner")), P()),
        out_specs=(rows, rows, rows),
        check_vma=False,
    )
```

```python
import functools

import jax
import jax.numpy as jnp
from jax import lax
from jax.experimental import pallas as pl
from jax.experimental.pallas import tpu as pltpu
from jax.sharding import PartitionSpec as P

F32 = jnp.float32
BF16 = jnp.bfloat16
MESH = pl.DeviceIdType.MESH
LOG2E = 1.4426950408889634
HIDDEN = 1e30

FAR = -1
STEPS = (
    (0, 0, 0),
    (1, 0, 1),
    (2, 0, 0),
    (2, 0, 1),
    (1, 1, 0),
    (1, 1, 1),
    (2, 1, 0),
    (2, 1, 1),
    (0, 1, 0),
    (1, 0, 0),
    (FAR, 1, 1),
    (FAR, 0, 1),
)
EVENTS = {
    1: (("in 10", "swap"),),
    2: (("in 20",),),
    4: (("in 11", "out 20"),),
    6: (("in 21", "out 11"),),
    8: (("in 01", "out 21"),),
    10: (("out 10",), ("in 31", "out 10", "out 01")),
    11: (("out 01",), ("in 30", "out 31")),
    12: ((), ("out 30",)),
}
FORWARD = {
    "11": ("10", 0, 1),
    "20": ("10", 1, 0),
    "21": ("20", 0, 1),
    "30": ("20", 1, 0),
    "31": ("21", 1, 0),
}
RETURN = {
    "01": "home",
    "10": "home",
    "11": "x",
    "20": "z",
    "21": "home",
    "30": "home",
    "31": "x",
}


def dot(a, b):
    return jnp.dot(a, b, preferred_element_type=F32)


def dot_nt(a, b):
    return lax.dot_general(a, b, (((1,), (1,)), ((), ())), preferred_element_type=F32)


def at_step(t, values):
    return sum(jnp.where(t == n, value, 0) for n, value in enumerate(values))


def kernel(
    sizes,
    q_hbm, k_hbm, v_hbm, o_hbm, g_hbm, norm_hbm, pos_hbm,
    dq_out, dk_out, dv_out,
    qs, gs, os, qt, gt, kv, norm, cols, cols_in, lse, delta, hidden,
    dq, dkv, staged, merged, home, dq_send, dq_recv, pos_ref,
    load_q, load_g, load_o, load_kv, load_norm, load_pos,
    swap_send, swap_recv, fwd_send, fwd_recv, ret_send, merge_recv, home_recv,
):
    n_outer, n_inner, heads, rows, hd = sizes
    shard = rows // 2
    scale = hd**-0.5
    outer, inner = lax.axis_index("outer"), lax.axis_index("inner")
    core = lax.rem(outer, 2)
    on_core0 = pl.when(core == 0)
    on_core1 = pl.when(core == 1)

    def chip(dc, e=0):
        return (
            lax.rem(outer + 2 * dc + n_outer, n_outer),
            lax.rem(inner + e + n_inner, n_inner),
        )

    sibling = (outer + 1 - 2 * core, inner)

    def remote(src, dst, send, recv, to):
        return pltpu.make_async_remote_copy(
            src_ref=src, dst_ref=dst, send_sem=send, recv_sem=recv,
            device_id=to, device_id_type=MESH,
        )

    def loads(src, dst, sem):
        return [
            pltpu.make_async_copy(
                src.at[:, pl.ds(h * hd, hd)], dst.at[pl.ds(h * rows, rows)], sem.at[h]
            )
            for h in range(heads)
        ]

    kv_loads = [
        pltpu.make_async_copy(ref, kv.at[0, n], load_kv.at[n])
        for n, ref in enumerate((k_hbm, v_hbm))
    ]
    pos_load = pltpu.make_async_copy(pos_hbm, pos_ref, load_pos)
    norm_load = pltpu.make_async_copy(norm_hbm, norm, load_norm)
    q_loads = loads(q_hbm, qs.at[0], load_q)
    g_loads = loads(g_hbm, gs.at[0], load_g)
    o_loads = loads(o_hbm, os, load_o)

    swap_q = remote(qs.at[0], qs.at[1], swap_send.at[0], swap_recv.at[0], sibling)
    swap_g = remote(gs.at[0], gs.at[1], swap_send.at[1], swap_recv.at[1], sibling)
    swap_cols = remote(cols, cols_in, swap_send.at[2], swap_recv.at[2], sibling)
    swap_dq = remote(dq_send, dq_recv, swap_send.at[3], swap_recv.at[3], sibling)

    def slot_of(name):
        return 2 * int(name[0]) + int(name[1])

    def on_core(name):
        return on_core1 if name[0] == "3" else lambda body: body()

    sources = {"10": ("own", 1, 0), "01": ("own", 0, 1), **FORWARD}

    def forward(name):
        source, dc, e = sources[name]
        src, dst = 0 if source == "own" else slot_of(source), slot_of(name)
        return remote(kv.at[src], kv.at[dst], fwd_send.at[dst], fwd_recv.at[dst], chip(dc, e))

    def send_on(source):
        for name, (before, _, _) in sources.items():
            if before == source:
                on_core(name)(lambda name=name: forward(name).start())

    def send_own():
        for name, (before, dc, e) in sources.items():
            if before == "own":
                dst = slot_of(name)
                for n, ref in enumerate((k_hbm, v_hbm)):
                    remote(
                        ref, kv.at[dst, n], fwd_send.at[dst], fwd_recv.at[dst], chip(dc, e)
                    ).start()

    def arrival(ref, sem, slot):
        return remote(ref.at[slot], ref.at[slot], fwd_send.at[slot], sem.at[slot], sibling)

    def onto(name):
        return {"home": "00", "x": name[0] + "0", "z": str(int(name[0]) - 1) + name[1]}[RETURN[name]]

    def back(name):
        slot = slot_of(name)
        if RETURN[name] == "home":
            ref, sem, to = home, home_recv, chip(-int(name[0]), -int(name[1]))
        else:
            ref, sem, to = merged, merge_recv, chip(-1) if RETURN[name] == "z" else chip(0, -1)
        return remote(staged.at[slot], ref.at[slot], ret_send.at[slot], sem.at[slot], to)

    barrier = pltpu.get_barrier_semaphore()

    def greet(device):
        pl.semaphore_signal(barrier, inc=1, device_id=device, device_id_type=MESH)

    reached = sorted({(dc, e) for _, dc, e in sources.values()})
    for dc, e in reached:
        greet(chip(-dc, -e))
    greet(sibling)
    for copy in (*kv_loads, *q_loads, *g_loads):
        copy.start()
    pl.semaphore_wait(barrier, 1 + len(reached))
    send_own()
    for copy in kv_loads:
        copy.wait()
    for copy in (*o_loads, norm_load, pos_load):
        copy.start()
    for copy in q_loads:
        copy.wait()
    swap_q.start()
    for copy in g_loads:
        copy.wait()
    swap_g.start()
    dkv[...] = jnp.zeros_like(dkv)
    dq[...] = jnp.zeros_like(dq)

    norm_load.wait()
    pos_load.wait()
    lane = lax.broadcasted_iota(jnp.int32, (rows, hd), 1)
    padded = jnp.concatenate([norm[...] * LOG2E, jnp.zeros((hd - heads, rows), F32)], 0)
    cols[0] = padded.T
    for copy in o_loads:
        copy.wait()
    packed = jnp.zeros((rows, hd), F32)
    for h in range(heads):
        part = pl.ds(h * rows, rows)
        product = gs[0, part, :].astype(F32) * os[part, :].astype(F32)
        packed = jnp.where(lane == h, jnp.sum(product, axis=1, keepdims=True), packed)
    cols[1] = packed
    swap_cols.start()

    def prepare(side, source):
        for h in range(heads):
            part = pl.ds(h * rows, rows)
            lse[side, part, :] = jnp.broadcast_to(source[0, :, h : h + 1], (rows, hd))
            delta[side, part, :] = jnp.broadcast_to(source[1, :, h : h + 1], (rows, hd))
            qt[side, :, part] = qs[side, part, :].T
            gt[side, :, part] = gs[side, part, :].T

    prepare(0, cols)

    def positions(outer_index, inner_index, dim):
        first = 2 * (outer_index * n_inner + inner_index)
        at = lax.broadcasted_iota(jnp.int32, (rows, rows), dim)
        start = jnp.where(at < shard, pos_ref[first], pos_ref[first + 1] - 1)
        return start * shard + at

    chunk = heads * rows // 2

    def step(side, dc, e):
        slot = 2 * dc + e
        q_pos = positions(outer + side * (1 - 2 * core), inner, 0)
        kv_outer, kv_inner = chip(-dc, -e)
        k_pos = positions(kv_outer, kv_inner, 1)
        hidden[...] = jnp.where(k_pos <= q_pos, 0.0, HIDDEN)
        k, v = kv[slot, 0], kv[slot, 1]

        def front(j):
            part = pl.ds(j * chunk, chunk)
            return dot_nt(qs[side, part, :], k), dot_nt(gs[side, part, :], v)

        def middle(j, s, dp):
            part = pl.ds(j * chunk, chunk)
            row_lse = jnp.tile(lse[side, part, :], (1, rows // hd))
            row_delta = jnp.tile(delta[side, part, :], (1, rows // hd))
            exponent = s * (scale * LOG2E) - row_lse
            exponent = exponent.reshape(-1, rows, rows) - hidden[...][None]
            weights = jnp.exp2(exponent.reshape(chunk, rows))
            score_grad = weights * (dp - row_delta) * scale
            return weights.astype(BF16), score_grad.astype(BF16)

        def back(j, weights, score_grad):
            part = pl.ds(j * chunk, chunk)
            dq[side, part, :] += dot(score_grad, k)
            return dot(qt[side, :, part], score_grad), dot(gt[side, :, part], weights)

        ahead = front(0)
        dk = dv = None
        for j in range(2):
            now, ahead = ahead, front(1) if j == 0 else None
            dk_part, dv_part = back(j, *middle(j, *now))
            dk, dv = (dk_part, dv_part) if j == 0 else (dk + dk_part, dv + dv_part)
        dkv[slot, 0] += dk
        dkv[slot, 1] += dv

    far = 3 * core

    def act(what):
        if what == "swap":
            swap_q.wait_recv()
            swap_g.wait_recv()
            swap_cols.wait_recv()
            prepare(1, cols_in)
            return
        kind, name = what.split()
        slot = slot_of(name)
        if kind == "in":
            arrival(kv, fwd_recv, slot).wait_recv()
            send_on(name)
            return
        total = dkv[slot]
        for other in [other for other in RETURN if onto(other) == name]:
            arrival(merged, merge_recv, slot_of(other)).wait_recv()
            total += merged[slot_of(other)].astype(F32)
        staged[slot] = total.astype(BF16)
        back(name).start()

    def events_at(n, here):
        if n not in EVENTS:
            return
        by_core = EVENTS[n]
        if len(by_core) == 1:
            pl.when(here)(lambda: [act(what) for what in by_core[0]] and None)
            return
        for index, events in enumerate(by_core):
            if events:
                pl.when(here & (core == index))(
                    lambda events=events: [act(what) for what in events] and None
                )

    def body(t, carry):
        for n in range(len(STEPS)):
            events_at(n, t == n)
        dc = at_step(t, [far if dc == FAR else dc for dc, _, _ in STEPS])
        e = at_step(t, [e for _, e, _ in STEPS])
        side = at_step(t, [side for _, _, side in STEPS])
        step(side, dc, e)
        return carry

    lax.fori_loop(0, len(STEPS), body, 0)

    events_at(len(STEPS), core >= 0)
    dq_send[...] = dq[1].astype(BF16)
    swap_dq.start()

    swap_dq.wait_recv()
    for h in range(heads):
        part = pl.ds(h * rows, rows)
        total = dq[0, part, :] + dq_recv[part, :].astype(F32)
        dq_out[:, h * hd : (h + 1) * hd] = total.astype(BF16)

    total = dkv[0]
    for name in RETURN:
        if RETURN[name] == "home" and name[0] != "3":
            arrival(home, home_recv, slot_of(name)).wait_recv()
            total += home[slot_of(name)].astype(F32)
    dkv[0] = total
    for name in RETURN:
        if RETURN[name] == "home" and name[0] == "3":

            @on_core1
            def _(slot=slot_of(name)):
                arrival(home, home_recv, slot).wait_recv()
                dkv[0] += home[slot].astype(F32)

    dk_out[...] = dkv[0, 0].T.astype(BF16)
    dv_out[...] = dkv[0, 1].T.astype(BF16)

    for copy in (swap_q, swap_g, swap_cols, swap_dq):
        copy.wait_send()
    for name in sources:

        @on_core(name)
        def _(name=name):
            forward(name).wait_send()
            back(name).wait_send()


def store(*refs):
    copies = [
        pltpu.make_async_copy(refs[n], refs[3 + n], refs[6].at[n]) for n in range(3)
    ]
    for copy in copies:
        copy.start()
    for copy in copies:
        copy.wait()


def local(mesh, queries, key_rows, value_rows, outputs, out_grad, log_norm, shard_pos):
    rows, hd = key_rows.shape
    heads = queries.shape[1] // hd
    flat = heads * rows
    sizes = (mesh.shape["outer"], mesh.shape["inner"], heads, rows, hd)
    dma = pltpu.SemaphoreType.DMA
    scratch = [
        pltpu.VMEM((2, flat, hd), BF16),
        pltpu.VMEM((2, flat, hd), BF16),
        pltpu.VMEM((flat, hd), BF16),
        pltpu.VMEM((2, hd, flat), BF16),
        pltpu.VMEM((2, hd, flat), BF16),
        pltpu.VMEM((8, 2, rows, hd), BF16),
        pltpu.VMEM((heads, rows), F32),
        pltpu.VMEM((2, rows, hd), F32),
        pltpu.VMEM((2, rows, hd), F32),
        pltpu.VMEM((2, flat, hd), F32),
        pltpu.VMEM((2, flat, hd), F32),
        pltpu.VMEM((rows, rows), F32),
        pltpu.VMEM((2, flat, hd), F32),
        pltpu.VMEM((8, 2, hd, rows), F32),
        pltpu.VMEM((8, 2, hd, rows), BF16),
        pltpu.VMEM((8, 2, hd, rows), BF16),
        pltpu.VMEM((8, 2, hd, rows), BF16),
        pltpu.VMEM((flat, hd), BF16),
        pltpu.VMEM((flat, hd), BF16),
        pltpu.SMEM(shard_pos.shape, jnp.int32),
        dma((heads,)),
        dma((heads,)),
        dma((heads,)),
        dma((2,)),
        dma,
        dma,
        dma((4,)),
        dma((4,)),
        dma((8,)),
        dma((8,)),
        dma((8,)),
        dma((8,)),
        dma((8,)),
    ]
    hbm = pl.BlockSpec(memory_space=pltpu.HBM)
    vmem = pl.BlockSpec(memory_space=pltpu.VMEM)
    grads = pl.pallas_call(
        functools.partial(kernel, sizes),
        out_shape=(
            pltpu.VMEM(queries.shape, BF16),
            pltpu.VMEM(key_rows.shape, BF16),
            pltpu.VMEM(value_rows.shape, BF16),
        ),
        in_specs=[hbm] * 7,
        out_specs=(vmem,) * 3,
        scratch_shapes=scratch,
        compiler_params=pltpu.CompilerParams(
            collective_id=0, has_side_effects=True, vmem_limit_bytes=56 * 2**20
        ),
        name="window_grads",
    )(queries, key_rows, value_rows, outputs, out_grad, log_norm, shard_pos)
    return pl.pallas_call(
        store,
        out_shape=[jax.ShapeDtypeStruct(grad.shape, grad.dtype) for grad in grads],
        in_specs=[vmem] * 3,
        out_specs=[hbm] * 3,
        scratch_shapes=[dma((3,))],
        name="store",
    )(*(pltpu.with_memory_space_constraint(grad, pltpu.VMEM) for grad in grads))


def solution(mesh):
    rows = P(("outer", "inner"), None)
    return jax.shard_map(
        functools.partial(local, mesh),
        mesh=mesh,
        in_specs=(rows, rows, rows, rows, rows, P(None, ("outer", "inner")), P()),
        out_specs=(rows, rows, rows),
        check_vma=False,
    )
```
